32 devices in a mesh: groups: 1, ex: 16 (over z, y, core), layer: 2 (over x), pb: 1.
Axes of the slice: x: 2, y: 2, z: 4, core: 2. Of those that a mesh axis runs over, the one named last changes fastest.
Arguments:
- train_grads: float32 [2, 1536, 1024], P('layer', ('groups', 'ex')), may hold values from -64 to 64
- query_grads: float32 [2, 1, 512, 1024], P('layer', 'pb', ('groups', 'ex')), may hold values from -64 to 64
- damping: float32 [2], P('layer'), may hold values from 0.05 to 0.5
Outputs:
- influence: float32 [1536, 1, 512], P(('groups', 'ex'), 'pb', 'layer')
The draws below stay inside these ranges and needn't reach their ends.
All inputs are finite; a program needn't handle non-finite values.
Results may differ from the reference program's by a relative error of at most 0.0003.
Values sent between devices are 32-bit elements; how exact they have to be, the bound alone decides.
No kernel may reach another device: no remote copies, remote signals or barrier semaphores. Data moves between devices by JAX's collectives and lax.ppermute only.
A program may use at most 64 MiB of HBM per device.

```python
import math
import jax
import jax.numpy as jnp
from jax import lax

P_SIZE = 1024
L = 2
NEX = 1536
QH = 1
NQE = 512


def column_scales(key):
    spread = jax.random.uniform(jax.random.fold_in(key, 101), (L, P_SIZE))
    return jnp.exp(jnp.log(0.1) + spread * jnp.log(30.0))


def gradient_law(key, row_total, salt_value):
    noise_key = jax.random.fold_in(key, salt_value)
    noise_field = jax.random.truncated_normal(noise_key, -4.0, 4.0, (L, row_total, P_SIZE))
    mixed_field = noise_field + 0.5 * jnp.roll(noise_field, 1, axis=2) - 0.35 * jnp.roll(noise_field, 5, axis=2)
    row_spread = jax.random.uniform(jax.random.fold_in(key, salt_value + 1), (L, row_total, 1))
    row_scale = jnp.exp(jnp.log(0.5) + row_spread * jnp.log(4.0))
    return mixed_field * row_scale * column_scales(key)[:, None, :]


def draw_train_grads(key, part):
    return gradient_law(key, NEX, 11).astype(jnp.float32)


def draw_query_grads(key, part):
    values = gradient_law(key, QH * NQE, 29) * (P_SIZE * L) ** (-0.5)
    return values.reshape(L, QH, NQE, P_SIZE).astype(jnp.float32)


def levels(rng, dims, shards, smallest, high):
    factor_of, own = 1.0, jax.random.fold_in(rng, 6)
    for axis_at, shards_of in shards:
        heights = jnp.exp(jax.random.uniform(jax.random.fold_in(own, axis_at), (shards_of,), jnp.float32, smallest / len(shards), high / len(shards)))
        factor_of = factor_of * jnp.repeat(heights, dims[axis_at] // shards_of).reshape([-1 if axis == axis_at else 1 for axis in range(len(dims))])
    return factor_of


def setup_inputs(seed: int = 0, part: int = 0) -> dict:
    seeds = jax.random.split(jax.random.key(seed), 4)
    part_splits = jax.random.split(jax.random.fold_in(seeds[3], part), 4)
    train_grads = draw_train_grads(jax.random.fold_in(jax.random.fold_in(seeds[3], part), 71), part)
    query_grads = draw_query_grads(jax.random.fold_in(jax.random.fold_in(seeds[3], part), 71), part)
    damping = jnp.clip(jnp.exp(math.log(0.5) - 2.3025851 * jax.random.uniform(seeds[2], (L,), jnp.float32) ** levels(seeds[2], (L,), ((0, 2),), -0.2, 0.2)), 0.05, 0.5)
    return dict(train_grads=train_grads, query_grads=query_grads, damping=damping)


def solve_rows(factor, rows_in):
    inner = lax.linalg.triangular_solve(factor, rows_in, left_side=False, lower=True, transpose_a=True)
    return lax.linalg.triangular_solve(factor, inner, left_side=False, lower=True, transpose_a=False)

def reference(train_grads, query_grads, damping):
    queries = query_grads.reshape(L, QH * NQE, P_SIZE)
    identity = jnp.eye(P_SIZE, dtype=jnp.float32)
    total = jnp.zeros((NEX, QH * NQE), jnp.float32)
    for layer_index in range(L):
        grads = train_grads[layer_index]
        gram_matrix = jnp.dot(grads.T.astype(jnp.float32), grads.astype(jnp.float32), precision=lax.Precision.HIGHEST, preferred_element_type=jnp.float32)
        fisher = gram_matrix / NEX + damping[layer_index] * identity
        factor = jnp.linalg.cholesky(fisher)
        solved = solve_rows(factor, queries[layer_index])
        total = total + jnp.dot(grads.astype(jnp.float32), solved.T.astype(jnp.float32), precision=lax.Precision.HIGHEST, preferred_element_type=jnp.float32)
    return total.reshape(NEX, QH, NQE)
```

```python
import functools
import jax
import jax.numpy as jnp
from jax import lax
from jax.experimental import pallas as pl
from jax.experimental.pallas import tpu as pltpu
from jax.sharding import PartitionSpec as P

LANES = 128
SUBL = 8
BLK = 128

def row_of(x, k):
    return jnp.broadcast_to(x[k:k + 1, :], x.shape)

def col_of(x, k):
    return jnp.broadcast_to(x[:, k:k + 1], x.shape)

def tree_sum(parts):
    while len(parts) > 1:
        nxt = [parts[a] + parts[a + 1] for a in range(0, len(parts) - 1, 2)]
        if len(parts) % 2:
            nxt.append(parts[-1])
        parts = nxt
    return parts[0]

def eliminate(dref, wv_put, t):
    gs = SUBL * t
    lane = lax.broadcasted_iota(jnp.int32, (SUBL, LANES), 1)
    sub = lax.broadcasted_iota(jnp.int32, (SUBL, LANES), 0)
    for g in range(BLK // gs):
        r0 = g * gs
        rows = [dref[r0 + SUBL * s:r0 + SUBL * s + SUBL, :] for s in range(t)]
        cols = [[col_of(rows[s], r0 + j) for s in range(t)] for j in range(gs)]
        inside = (lane >= r0) & (lane < r0 + gs)
        rows = [jnp.where(inside, jnp.where(lane == r0 + SUBL * s + sub, 1.0, 0.0), rows[s]) for s in range(t)]
        done = lane < r0 + gs
        for s in range(t):
            wv_put(0, r0 + SUBL * s, jnp.where(done, rows[s], 0.0))
        pivot = row_of(cols[0][0], 0)
        for k in range(gs):
            sk, kk = divmod(k, SUBL)
            inv = 1.0 / pivot
            if k + 1 < gs:
                s1, k1 = divmod(k + 1, SUBL)
                cross = row_of(cols[k][s1], k1) * row_of(cols[k + 1][sk], kk)
                pivot = row_of(cols[k + 1][s1], k1) - cross * inv
            isk = sub == kk
            pr = row_of(rows[sk], kk) * inv
            for s in range(t):
                new = rows[s] - cols[k][s] * pr
                rows[s] = jnp.where(isk, pr, new) if s == sk else new
            for j in range(k + 1, gs):
                pe = row_of(cols[j][sk], kk) * inv
                for s in range(t):
                    new = cols[j][s] - cols[k][s] * pe
                    cols[j][s] = jnp.where(isk, pe, new) if s == sk else new
        for s in range(t):
            wv_put(1, r0 + SUBL * s, jnp.where(done, rows[s], 0.0))
        if g + 1 < BLK // gs:
            v = [row_of(rows[m // SUBL], m % SUBL) for m in range(gs)]
            for i in range(g * t + t, BLK // SUBL):
                c = dref[SUBL * i:SUBL * i + SUBL, :]
                parts = [col_of(c, r0 + m) * v[m] for m in range(gs)]
                dref[SUBL * i:SUBL * i + SUBL, :] = jnp.where(inside, 0.0, c) - tree_sum(parts)

def split2(x):
    hi = x.astype(jnp.bfloat16)
    lo = (x - hi.astype(jnp.float32)).astype(jnp.bfloat16)
    return hi, lo

def left3(x):
    hi, lo = split2(x)
    return jnp.concatenate([hi, hi, lo], axis=1)

def right3(x):
    hi, lo = split2(x)
    return jnp.concatenate([hi, lo, hi], axis=1)

def dot_nt(a, b):
    return lax.dot_general(a, b, (((1,), (1,)), ((), ())), preferred_element_type=jnp.float32)


def gram_kernel(half_ref, rows_ref, out_ref, left_ref, right_ref):
    turned = rows_ref[...].T
    hi, lo = split2(turned)
    left_ref[...] = jnp.concatenate([hi, hi, lo], axis=1)
    right_ref[...] = jnp.concatenate([hi, lo, hi], axis=1)
    half = BLK // 2
    first = half_ref[0] * half
    at = 0
    for i in range(rows_ref.shape[1] // BLK):
        mine = left_ref[pl.ds(pl.multiple_of(i * BLK + first, half), half), :]
        strip = dot_nt(mine, right_ref[0:(i + 1) * BLK, :])
        for j in range(i + 1):
            out_ref[at:at + half, :] = strip[:, j * BLK:(j + 1) * BLK]
            at += half


def gram_half(which, rows):
    n, coords = rows.shape
    nblk = coords // BLK
    return pl.pallas_call(
        gram_kernel,
        out_shape=jax.ShapeDtypeStruct((nblk * (nblk + 1) // 2 * (BLK // 2), LANES), jnp.float32),
        in_specs=[pl.BlockSpec(memory_space=pltpu.SMEM), pl.BlockSpec(memory_space=pltpu.VMEM)],
        out_specs=pl.BlockSpec(memory_space=pltpu.VMEM),
        scratch_shapes=[pltpu.VMEM((coords, 3 * n), jnp.bfloat16)] * 2,
        compiler_params=pltpu.CompilerParams(vmem_limit_bytes=40 * 2**20),
        name="gram_half",
    )(which, rows)


def factor_kernel(scale, t, half_ref, damp_ref, own_ref, other_ref, t_ref, q_ref, out_ref, m_ref, wv_ref, y_ref, z_ref):
    coords = t_ref.shape[1]
    nt, nq = t_ref.shape[0], q_ref.shape[0]
    parts = out_ref.shape[0]
    nblk = coords // BLK
    half = BLK // 2
    lane = lax.broadcasted_iota(jnp.int32, (half, LANES), 1)
    sub = lax.broadcasted_iota(jnp.int32, (half, LANES), 0)
    damp = damp_ref[0]
    at = 0
    for i in range(nblk):
        for j in range(i + 1):
            for which, src in ((half_ref[0], own_ref), (1 - half_ref[0], other_ref)):
                first = pl.multiple_of(which * half, half)
                x = src[at:at + half, :] * scale
                if i == j:
                    x = x + jnp.where(lane == sub + first, damp, 0.0)
                m_ref[pl.ds(i * BLK + first, half), j * BLK:(j + 1) * BLK] = x
            at += half
    t0, q0 = coords, coords + nt
    m_ref[t0:q0, :] = t_ref[...]
    m_ref[q0:q0 + nq, :] = q_ref[...]
    total = coords + nt + nq
    for k in range(nblk):
        c0, c1 = k * BLK, (k + 1) * BLK
        slot = k % 2

        def put(which, r, x, slot=slot):
            wv_ref[slot, which * BLK + r:which * BLK + r + SUBL, :] = x

        eliminate(m_ref.at[c0:c1, c0:c1], put, t)
        wv = right3(wv_ref[slot])

        def panel(r0, r1):
            yz = dot_nt(left3(m_ref[r0:r1, c0:c1]), wv)
            y_ref[slot, r0:r1, :] = left3(yz[:, :BLK])
            z_ref[slot, r0:r1, :] = right3(yz[:, BLK:])

        def update(r0, r1, a, b):
            m_ref[r0:r1, a:b] -= dot_nt(y_ref[slot, r0:r1, :], z_ref[slot, a:b, :])

        if k + 1 < nblk:
            panel(c1, c1 + BLK)
            update(c1, c1 + BLK, c1, c1 + BLK)
            panel(c1 + BLK, total)
            update(c1 + BLK, total, c1, c1 + BLK)
            for a in range(c1 + BLK, coords, 2 * BLK):
                b = min(a + 2 * BLK, coords)
                update(a, total, a, b)
        else:
            panel(c1, total)
        s = dot_nt(y_ref[slot, t0:q0, :], z_ref[slot, q0:q0 + nq, :])
        for part in range(parts):
            piece = s[:, part * (nq // parts):(part + 1) * (nq // parts)]
            if k == 0:
                out_ref[part] = piece
            else:
                out_ref[part] += piece


def factor_score(which, damping, own, other, rows, queries, total_rows, parts):
    coords = rows.shape[1]
    nt, nq = rows.shape[0], queries.shape[0]
    total = coords + nt + nq
    vmem = pl.BlockSpec(memory_space=pltpu.VMEM)
    smem = pl.BlockSpec(memory_space=pltpu.SMEM)
    return pl.pallas_call(
        functools.partial(factor_kernel, 1.0 / total_rows, 2),
        out_shape=jax.ShapeDtypeStruct((parts, nt, nq // parts), jnp.float32),
        in_specs=[smem, smem] + [vmem] * 4,
        out_specs=vmem,
        scratch_shapes=[
            pltpu.VMEM((total, coords), jnp.float32),
            pltpu.VMEM((2, 2 * BLK, BLK), jnp.float32),
            pltpu.VMEM((2, total, 3 * BLK), jnp.bfloat16),
            pltpu.VMEM((2, total, 3 * BLK), jnp.bfloat16),
        ],
        compiler_params=pltpu.CompilerParams(vmem_limit_bytes=56 * 2**20),
        name="factor_score",
    )(which, damping, own, other, rows, queries)


def swap(x, axis, bit):
    return lax.ppermute(x, axis, [(i, i ^ (1 << bit)) for i in range(lax.axis_size(axis))])


def bit_of(axis, bit):
    return (lax.axis_index(axis) >> bit) & 1


def halve(x, axis, bit):
    pair = x.reshape(2, -1, x.shape[-1])
    mine = bit_of(axis, bit)
    return pair[mine] + swap(pair[1 - mine], axis, bit)


def double(x, axis, bit):
    got = swap(x, axis, bit)
    low = bit_of(axis, bit) == 0
    return jnp.concatenate([jnp.where(low, x, got), jnp.where(low, got, x)], axis=0)


def sum_over(x, axis, bits):
    if len(bits) < 2:
        for bit in bits:
            x = halve(x, axis, bit)
        for bit in reversed(bits):
            x = double(x, axis, bit)
        return x
    one, two, rest = bits[0], bits[1], bits[2:]
    n = x.shape[0] // 2
    a, b = x[:n], x[n:]
    a, b = halve(a, axis, one), halve(b, axis, two)
    a, b = halve(a, axis, two), halve(b, axis, one)
    both = jnp.concatenate([a.reshape(2, -1, x.shape[-1]), b.reshape(2, -1, x.shape[-1])], axis=1)
    both = both.reshape(-1, x.shape[-1])
    for bit in rest:
        both = halve(both, axis, bit)
    for bit in reversed(rest):
        both = double(both, axis, bit)
    both = both.reshape(2, -1, x.shape[-1])
    m = both.shape[1] // 2
    a, b = both[:, :m].reshape(-1, x.shape[-1]), both[:, m:].reshape(-1, x.shape[-1])
    a, b = double(a, axis, two), double(b, axis, one)
    a, b = double(a, axis, one), double(b, axis, two)
    return jnp.concatenate([a, b], axis=0)


def on_device(train_grads, query_grads, damping):
    rows = train_grads[0]
    shards = lax.axis_size("ex")
    layers = lax.axis_size("layer")
    bits = list(range(shards.bit_length() - 1))
    queries = lax.all_gather(query_grads[0, 0], "ex", axis=0, tiled=True)
    if lax.axis_size("pb") == 2:
        pair, pair_rows = ("pb", 0), rows
    else:
        pair = ("ex", bits.pop(0))
        pair_rows = jnp.concatenate([rows, swap(rows, *pair)], axis=0)
    which = bit_of(*pair).reshape(1)
    own = sum_over(gram_half(which, pair_rows), "ex", bits)
    other = swap(own, *pair)
    scores = factor_score(which, damping, own, other, rows, queries, rows.shape[0] * shards, layers)
    me = lax.axis_index("layer")
    share = scores[me]
    for step in range(1, layers):
        to = [(i, (i + step) % layers) for i in range(layers)]
        share = share + lax.ppermute(scores[(me + step) % layers], "layer", to)
    return share[:, None, :]


def solution(mesh):
    in_specs = (
        P("layer", ("groups", "ex"), None),
        P("layer", "pb", ("groups", "ex"), None),
        P("layer"),
    )
    out_specs = P(("groups", "ex"), "pb", "layer")
    return jax.shard_map(
        on_device, mesh=mesh, in_specs=in_specs, out_specs=out_specs, check_vma=False
    )
```
